256 devices in a mesh: ctx: 64 (over y_lo, x, z), head: 4 (over y_hi, core).
Axes of the slice: x: 4, y: 4 (y_hi: 2, y_lo: 2; y = y_hi * 2 + y_lo), z: 8, core: 2. Of those that a mesh axis runs over, the one named last changes fastest.
Arguments:
- queries: bfloat16 [1, 16384, 2048], P(None, 'ctx', 'head'), may hold values from -128 to 128
- key_rows: bfloat16 [1, 16384, 128], P(None, ('ctx', 'head')), may hold values from -4.5 to 4.5
- value_rows: bfloat16 [1, 16384, 128], P(None, ('ctx', 'head')), may hold values from -5 to 5
- document_lengths: int32 [1, 4], replicated, may hold values from 1 to 12288, 16384 in all within a row
Outputs:
- attended: bfloat16 [1, 16384, 2048], P(None, 'ctx', 'head')
The draws below stay inside these ranges and needn't reach their ends.
All inputs are finite; a program needn't handle non-finite values.
Results may differ from the reference program's by a relative error of at most 0.0045.
Values may be sent and summed in bfloat16 or wider, within the bound.
A program may use at most 64 MiB of HBM per device.

```python
import math
import jax
import jax.numpy as jnp
import numpy as np
from jax import lax

HD = 128
HEADS = 16
SEQS = 1
NDOC = 4
LEN = 16384
MOST = 12288


def shared_base(key):
    base = jax.random.normal(key, (SEQS, LEN, HD), jnp.float32)
    return jnp.clip(base, -4.5, 4.5)


def draw_key_rows(key, part):
    base = shared_base(key)
    return base.astype(jnp.bfloat16)


def draw_queries(key, part):
    key = jax.random.fold_in(key, 3)
    noise = 3.0 * jnp.clip(jax.random.normal(key, (SEQS, LEN, HEADS, HD), jnp.float32), -4.5, 4.5)
    return noise.reshape(SEQS, LEN, HEADS * HD).astype(jnp.bfloat16)


def levels(stream_key, extent, cuts, least, top_value):
    factor_of, own = 1.0, jax.random.fold_in(stream_key, 6)
    for position, blocks in cuts:
        heights = jnp.exp(jax.random.uniform(jax.random.fold_in(own, position), (blocks,), jnp.float32, least / len(cuts), top_value / len(cuts)))
        factor_of = factor_of * jnp.repeat(heights, extent[position] // blocks).reshape([-1 if axis == position else 1 for axis in range(len(extent))])
    return factor_of


def split_up(count, total, reach, slope):
    portions = [(1 << 20) // math.isqrt(grade ** slope) + 1 for grade in range(2, count + 1)]
    spare, holding = total - reach - (count - 1), [1] * (count - 1)
    while spare > 0:
        movable = [i for i in range(count - 1) if holding[i] < reach]
        pool, remaining = sum([portions[i] for i in movable]), spare
        for i in movable:
            extra = min(reach - holding[i], max(1, remaining * portions[i] // pool), spare)
            holding[i] = holding[i] + extra
            spare = spare - extra
    return np.array([reach] + holding)


def uneven_parts(rng, count, total, bound, lean):
    if count == 2:
        one = jax.random.randint(rng, (), max(1, total - bound), min(bound, total - 1) + 1)
        return jnp.stack([one, total - one])
    tallies = jnp.asarray(split_up(count, total, bound, lean), jnp.int32)
    couples = (count - 1) // 2
    donor, taker = tallies[1:1 + 2 * couples:2], tallies[2:2 + 2 * couples:2]
    room = jnp.minimum(donor - 1, bound - taker)
    passed = jax.random.randint(jax.random.fold_in(rng, 1), (couples,), 0, 1 << 20) % (room + 1)
    tallies = tallies.at[1:1 + 2 * couples:2].set(donor - passed).at[2:2 + 2 * couples:2].set(taker + passed)
    return tallies[jax.random.permutation(jax.random.fold_in(rng, 2), count)]


def scatter_about(key, shape, spread, most, shards=(), held_as=jnp.bfloat16):
    loudness = levels(key, shape, shards, -0.22, 0.18) if shards else 1.0
    result = jax.random.normal(key, shape, jnp.float32) * spread * loudness
    return jnp.minimum(jnp.maximum(result, -most), most).astype(held_as)


def setup_inputs(seed: int = 0) -> dict:
    key_of = jax.random.split(jax.random.key(seed), 5)
    queries = draw_queries(jax.random.fold_in(key_of[4], 71), 0)
    key_rows = draw_key_rows(jax.random.fold_in(key_of[4], 71), 0)
    value_rows = scatter_about(key_of[2], (SEQS, LEN, HD), 1.0, 5.0, ((1, 256),))
    document_lengths = jax.vmap(lambda own: uneven_parts(own, NDOC, LEN, MOST, 2))(jax.random.split(key_of[3], SEQS)).reshape((SEQS, NDOC)).astype(jnp.int32)
    return {"queries": queries, "key_rows": key_rows, "value_rows": value_rows, "document_lengths": document_lengths}


NEG = -1e+30

def document_ids(positions, ends):
    return lax.optimization_barrier(jnp.sum((positions[:, None] >= ends[None, :]).astype(jnp.int32), axis=1))

def reference(queries, key_rows, value_rows, document_lengths):
    scale = 1.0 / math.sqrt(HD)
    block_rows = math.gcd(LEN, 512)
    blocks = LEN // block_rows
    results = []
    for seq_index in range(SEQS):
        ends = jnp.cumsum(document_lengths[seq_index]).astype(jnp.int32)
        positions = jnp.arange(LEN, dtype=jnp.int32)
        key_docs = document_ids(positions, ends)
        keys_here = key_rows[seq_index]
        values_here = value_rows[seq_index]
        query_blocks = queries[seq_index].reshape(blocks, block_rows, HEADS, HD)
        query_blocks = query_blocks.transpose(0, 2, 1, 3).reshape(blocks * HEADS, block_rows, HD)
        starts = jnp.arange(blocks * HEADS, dtype=jnp.int32) // HEADS * block_rows

        def attend(item):
            query_block, start = item
            query_pos = start + jnp.arange(block_rows, dtype=jnp.int32)
            query_docs = document_ids(query_pos, ends)
            scores = jnp.dot(query_block, keys_here.T, preferred_element_type=jnp.float32) * scale
            valid = (positions[None, :] <= query_pos[:, None]) & (key_docs[None, :] == query_docs[:, None])
            scores = jnp.where(valid, scores, NEG)
            top = lax.optimization_barrier(jnp.max(scores, axis=1, keepdims=True))
            weights = jnp.where(valid, jnp.exp(scores - top), 0.0)
            total = lax.optimization_barrier(jnp.sum(weights, axis=1, keepdims=True))
            mixed = jnp.dot(weights.astype(jnp.bfloat16), values_here, preferred_element_type=jnp.float32)
            return (mixed / total).astype(jnp.bfloat16)
        output = lax.map(attend, (query_blocks, starts))
        output = output.reshape(blocks, HEADS, block_rows, HD).transpose(0, 2, 1, 3)
        results.append(output.reshape(LEN, HEADS * HD))
    return jnp.stack(results)
```

```python
import functools
import math

import jax
import jax.numpy as jnp
from jax import lax
from jax.experimental import pallas as pl
from jax.experimental.pallas import tpu as pltpu
from jax.sharding import PartitionSpec as P

MESH = pl.DeviceIdType.MESH
HIDE = -(2.0**100)
SCALE = math.log2(math.e) / math.sqrt(128.0)
ROWS = 256
HEADS = 4
WIDE = ROWS * HEADS
KEYS = 256
GROUPS = 8
STEPS = 2 * GROUPS


def device_at(y, x, z, core):
    return ((y % 2) * 32 + x * 8 + z, (y // 2) * 2 + core)


def kernel(
    lengths, q_ref, k_ref, v_ref, o_ref,
    kv, dk, qa, q2, score_a, score_b, acc, top, total, best_a, best_b, o_out, o_in, s_out, s_in,
    y_send, y_recv, x_send, x_recv, vz_send, vz_recv, r_send, r_recv, l_send, l_recv,
    core_send, core_recv, pair_send, pair_recv,
):
    ctx = lax.axis_index("ctx")
    head = lax.axis_index("head")
    y_lo, x, z = ctx // 32, (ctx // 8) % 4, ctx % 8
    y_hi, core = head // 2, head % 2
    y = y_hi * 2 + y_lo
    sibling = device_at(y, x, z, 1 - core)
    partner = device_at(y + 1 - 2 * y_lo, 3 - x, z, core)

    barrier = pltpu.get_barrier_semaphore()
    friends = [
        device_at((y + dy) % 4, x, z, (core + dc) % 2) for dy in range(4) for dc in range(2) if dy + dc > 0
    ]
    friends += [device_at(y, (x + dx) % 4, z, core) for dx in range(1, 4)]
    friends += [device_at(y, x, (z + dz) % 8, core) for dz in range(1, 8)]
    friends += [partner]
    for friend in friends:
        pl.semaphore_signal(barrier, inc=1, device_id=friend, device_id_type=MESH)

    starts, ends, run = [], [], jnp.int32(0)
    for d in range(4):
        starts.append(run)
        run = run + lengths[0, d]
        ends.append(run)

    def fill_queries(which, source):
        late = jnp.where(which == 0, y_lo, 1 - y_lo)
        own_x = jnp.where(which == 0, x, 3 - x)
        block = late * 32 + own_x * 8 + z
        pos = block * ROWS + lax.broadcasted_iota(jnp.int32, (ROWS, 128), 0)
        lane = lax.broadcasted_iota(jnp.int32, (ROWS, 128), 1)
        hide = lane - 64 > block
        for d in range(4):
            inside = (pos >= starts[d]) & (pos < ends[d])
            hide = hide | ((lane == d) & jnp.logical_not(inside))
        extra = jnp.where(hide, HIDE, 0.0).astype(jnp.bfloat16)
        for h in range(HEADS):
            qa[which, h * ROWS : (h + 1) * ROWS, 0:128] = source[:, h * 128 : (h + 1) * 128]
            qa[which, h * ROWS : (h + 1) * ROWS, 128:256] = extra

    def fill_keys(index, carry):
        group, late = index // 2, index % 2
        row = lax.broadcasted_iota(jnp.int32, (512, 128), 0)
        lane = lax.broadcasted_iota(jnp.int32, (512, 128), 1)
        block = late * 32 + (row // 128) * 8 + group
        pos = block * ROWS + ((row // 64) % 2) * 128 + y_lo * 64 + row % 64
        show = lane - 64 == block
        for d in range(4):
            show = show | ((lane == d) & (pos >= starts[d]) & (pos < ends[d]))
        dk[group, late] = jnp.where(show, 1.0, 0.0).astype(jnp.bfloat16)
        return carry

    fill_queries(0, q_ref)
    lax.fori_loop(0, 2 * GROUPS, fill_keys, 0)
    acc[...] = jnp.zeros_like(acc)
    total[...] = jnp.zeros_like(total)
    top[...] = jnp.full_like(top, -1e38)
    pl.semaphore_wait(barrier, len(friends))

    def y_copy(kind, turn):
        rows = kv.at[kind, z, y_lo, pl.ds(x * 128 + y_hi * 64, 64), :]
        return pltpu.make_async_remote_copy(
            src_ref=(k_ref, v_ref)[kind], dst_ref=rows, send_sem=y_send.at[kind, turn], recv_sem=y_recv.at[y],
            device_id=device_at(core + 2 * turn, x, z, kind), device_id_type=MESH,
        )

    def y_stay(kind):
        rows = kv.at[kind, z, y_lo, pl.ds(x * 128 + y_hi * 64, 64), :]
        return pltpu.make_async_copy((k_ref, v_ref)[kind], rows, y_recv.at[y])

    for kind in range(2):
        for turn in range(2):
            here = (core + 2 * turn == y) & (core == kind)
            pl.when(here)(lambda kind=kind: y_stay(kind).start())
            pl.when(jnp.logical_not(here))(lambda kind=kind, turn=turn: y_copy(kind, turn).start())

    pair_q = pltpu.make_async_remote_copy(
        src_ref=q_ref, dst_ref=q2, send_sem=pair_send.at[0], recv_sem=pair_recv.at[0],
        device_id=partner, device_id_type=MESH,
    )
    pair_o = pltpu.make_async_remote_copy(
        src_ref=o_out, dst_ref=o_in, send_sem=pair_send.at[1], recv_sem=pair_recv.at[1],
        device_id=partner, device_id_type=MESH,
    )
    pair_s = pltpu.make_async_remote_copy(
        src_ref=s_out, dst_ref=s_in, send_sem=pair_send.at[2], recv_sem=pair_recv.at[2],
        device_id=partner, device_id_type=MESH,
    )

    def z_of(g):
        far = (g + 1) // 2
        return (z + 8 + jnp.where(g % 2 == 1, -far, far)) % 8

    def column(at_x, at_z):
        return kv.at[core, at_z, :, pl.ds(at_x * 128, 128), :]

    def x_copy(g, dx):
        part = column(x, z_of(g))
        return pltpu.make_async_remote_copy(
            src_ref=part, dst_ref=part, send_sem=x_send.at[g, dx], recv_sem=x_recv.at[g, dx],
            device_id=device_at(y, (x + dx) % 4, z, core), device_id_type=MESH,
        )

    def x_wait(g, dx):
        part = column((x + 4 - dx) % 4, z_of(g))
        pltpu.make_async_copy(part, part, x_recv.at[g, dx]).wait()

    def vz_copy(dz):
        part = column(x, z)
        return pltpu.make_async_remote_copy(
            src_ref=part, dst_ref=part, send_sem=vz_send.at[dz], recv_sem=vz_recv.at[dz],
            device_id=device_at(y, x, (z + dz) % 8, core), device_id_type=MESH,
        )

    def ring_copy(way, hop):
        at = (z + 8 + jnp.where(way == 0, -hop, hop)) % 8
        part = kv.at[0, at] if hop < 3 else kv.at[0, at, way]
        send, recv = ((r_send, r_recv), (l_send, l_recv))[way]
        return pltpu.make_async_remote_copy(
            src_ref=part, dst_ref=part, send_sem=send.at[hop], recv_sem=recv.at[hop],
            device_id=device_at(y, x, (z + (1, 7)[way]) % 8, core), device_id_type=MESH,
        )

    def ring_wait(way, hop):
        at = (z + 8 + jnp.where(way == 0, -hop - 1, hop + 1)) % 8
        part = kv.at[0, at] if hop < 3 else kv.at[0, at, way]
        pltpu.make_async_copy(part, part, (r_recv, l_recv)[way].at[hop]).wait()

    def core_copy(g):
        part = kv.at[core, z_of(g)]
        return pltpu.make_async_remote_copy(
            src_ref=part, dst_ref=part, send_sem=core_send.at[g], recv_sem=core_recv.at[g],
            device_id=sibling, device_id_type=MESH,
        )

    def core_wait(g):
        part = kv.at[1 - core, z_of(g)]
        pltpu.make_async_copy(part, part, core_recv.at[g]).wait()

    def relay_values(g):
        dz = (z + 8 - z_of(g)) % 8
        part = column(x, z_of(g))
        pltpu.make_async_copy(part, part, vz_recv.at[dz]).wait()
        for dx in range(1, 4):
            x_copy(g, dx).start()

    def arrive(g):
        for hop in range(3):
            for way in range(2):

                @pl.when((core == 0) & (g == 2 * hop + 1 + way))
                def _():
                    ring_wait(way, hop)
                    ring_copy(way, hop + 1).start()

        @pl.when((core == 0) & (g == 7))
        def _():
            ring_wait(0, 3)
            ring_wait(1, 3)

        @pl.when(core == 1)
        def _():
            for dx in range(1, 4):
                x_wait(g, dx)

        core_copy(g).start()

        @pl.when((core == 1) & (g == 1))
        def _():
            relay_values(jnp.int32(3))
            relay_values(jnp.int32(4))

        @pl.when((core == 1) & (g == 2))
        def _():
            relay_values(jnp.int32(5))
            relay_values(jnp.int32(6))

        @pl.when((core == 1) & (g == 3))
        def _():
            relay_values(jnp.int32(7))

        core_wait(g)

    zero = jnp.int32(0)
    for yy in range(4):
        rows = kv.at[core, z, yy % 2, pl.ds(x * 128 + (yy // 2) * 64, 64), :]
        pltpu.make_async_copy(k_ref, rows, y_recv.at[yy]).wait()
    for dx in range(1, 4):
        x_copy(zero, dx).start()

    @pl.when(core == 1)
    def _():
        for dz in (1, 7, 2, 6, 3, 5, 4):
            vz_copy(dz).start()

    pair_q.start()
    for dx in range(1, 4):
        x_wait(zero, dx)

    @pl.when(core == 0)
    def _():
        ring_copy(0, 0).start()
        ring_copy(1, 0).start()

    core_copy(zero).start()

    @pl.when(core == 1)
    def _():
        relay_values(jnp.int32(1))
        relay_values(jnp.int32(2))

    core_wait(zero)

    def step_of(i):
        even_set = jnp.where((i >= 4) & (i < 12), 1, 0)
        even_group = jnp.where(i < 4, i, jnp.where(i < 12, i - 4, i - 8))
        odd_set = jnp.where((i < 2) | (i == 5) | (i == 8) | (i >= 12), 0, 1)
        odd_group = jnp.where(
            i < 2, i,
            jnp.where(i < 5, i - 2, jnp.where(i == 5, 2, jnp.where(i < 8, i - 3, jnp.where(i == 8, 3, jnp.where(i < 12, i - 4, i - 8))))),
        )
        which = jnp.where(y_lo == 0, even_set, odd_set)
        g = jnp.where(y_lo == 0, even_group, odd_group)
        return which, g

    def units_of(which, g):
        late = jnp.where(which == 0, y_lo, 1 - y_lo)
        own_x = jnp.where(which == 0, x, 3 - x)
        blocks = own_x + jnp.where(z_of(g) <= z, 1, 0)
        count = (blocks + 1) // 2
        return jnp.where(late == 1, 2 + count, jnp.maximum(count, 1))

    def locate(i, j):
        which, g = step_of(i)
        over = i >= STEPS
        which = jnp.where(over, y_lo, which)
        group = jnp.where(over, z, z_of(g))
        late = jnp.where(over, 1, j // 2)
        row = pl.multiple_of(jnp.where(over, 0, (j % 2) * KEYS), KEYS)
        return which, group, late, row

    def advance(i, j):
        which, g = step_of(i)
        more = (j + 1 < units_of(which, g)) & (i < STEPS)
        return jnp.where(more, i, jnp.minimum(i + 1, STEPS)), jnp.where(more, j + 1, 0)

    def prepare(i, j, got):
        which, g = step_of(i)
        first = (j == 0) & (i < STEPS)
        fresh = first & (g == got)
        pl.when(fresh)(lambda: arrive(g))

        @pl.when(first & (which == 1) & (g == 0))
        def _():
            pair_q.wait_recv()
            fill_queries(1, q2)

        return jnp.where(fresh, got + 1, got)

    def scores_of(i, j, score, best):
        which, group, late, row = locate(i, j)
        keys = jnp.concatenate([kv[0, group, late, pl.ds(row, KEYS), :], dk[group, late, pl.ds(row, KEYS), :]], axis=1)
        s = lax.dot_general(keys, qa[which], (((1,), (1,)), ((), ())), preferred_element_type=jnp.float32)
        score[...] = s
        best[...] = jnp.max(s, axis=0, keepdims=True)

    def diagonal(i, j, score, best):
        which, g = step_of(i)

        @pl.when((i < STEPS) & (g == 0) & (j + 1 == units_of(which, g)))
        def _():
            late = jnp.where(which == 0, y_lo, 1 - y_lo)
            own_x = jnp.where(which == 0, x, 3 - x)
            row = lax.broadcasted_iota(jnp.int32, (KEYS, WIDE), 0) + (j % 2) * KEYS
            key_pos = ((j // 2) * 32 + (row // 128) * 8 + z) * ROWS + ((row // 64) % 2) * 128 + y_lo * 64 + row % 64
            query_pos = (late * 32 + own_x * 8 + z) * ROWS + lax.broadcasted_iota(jnp.int32, (KEYS, WIDE), 1) % ROWS
            s = jnp.where(key_pos <= query_pos, score[...], HIDE)
            score[...] = s
            best[...] = jnp.max(s, axis=0, keepdims=True)

    def soften(i, j, score, best):
        which, group, late, row = locate(i, j)
        old = top[which]
        new = jnp.maximum(old, best[...])
        weights = jnp.exp2((score[...] - new) * SCALE)
        factor = jnp.exp2((old - new) * SCALE)
        top[which] = new
        total[which] = total[which] * factor + jnp.sum(weights, axis=0, keepdims=True)
        values = kv[1, group, late, pl.ds(row, KEYS), :]
        mixed = lax.dot_general(
            values, weights.astype(jnp.bfloat16), (((0,), (0,)), ((), ())), preferred_element_type=jnp.float32
        )
        acc[which] = acc[which] * factor + mixed

    def hand_back(i, j):
        which, g = step_of(i)

        @pl.when((i < STEPS) & (which == 1) & (g == GROUPS - 1) & (j + 1 == units_of(which, g)))
        def _():
            o_out[...] = (acc[1] / total[1]).astype(jnp.bfloat16)
            s_out[0:1, :] = top[1]
            s_out[1:2, :] = total[1]
            pair_o.start()
            pair_s.start()

    def two_units(turn, state):
        i, j, got = state
        i_b, j_b = advance(i, j)
        got = prepare(i_b, j_b, got)
        scores_of(i_b, j_b, score_b, best_b)
        soften(i, j, score_a, best_a)
        diagonal(i_b, j_b, score_b, best_b)
        hand_back(i, j)
        i_c, j_c = advance(i_b, j_b)
        got = prepare(i_c, j_c, got)
        scores_of(i_c, j_c, score_a, best_a)
        soften(i_b, j_b, score_b, best_b)
        diagonal(i_c, j_c, score_a, best_a)
        hand_back(i_b, j_b)
        return i_c, j_c, got

    units = jnp.int32(0)
    for which in range(2):
        for g in range(GROUPS):
            units = units + units_of(jnp.int32(which), jnp.int32(g))
    scores_of(zero, zero, score_a, best_a)
    diagonal(zero, zero, score_a, best_a)
    lax.fori_loop(0, (units + 1) // 2, two_units, (zero, zero, jnp.int32(1)))

    pair_o.wait_recv()
    pair_s.wait_recv()
    peak = jnp.maximum(top[0], s_in[0:1, :])
    mine = jnp.exp2((top[0] - peak) * SCALE)
    other = jnp.exp2((s_in[0:1, :] - peak) * SCALE) * s_in[1:2, :]
    whole = mine * total[0] + other
    mine, other = mine / whole, other / whole
    for h in range(HEADS):
        part = slice(h * ROWS, (h + 1) * ROWS)
        merged = acc[0, :, part] * mine[:, part] + o_in[:, part].astype(jnp.float32) * other[:, part]
        o_ref[:, h * 128 : (h + 1) * 128] = merged.T.astype(jnp.bfloat16)

    for kind in range(2):
        for turn in range(2):
            away = (core + 2 * turn != y) | (core != kind)
            pl.when(away)(lambda kind=kind, turn=turn: y_copy(kind, turn).wait_send())
    for dx in range(1, 4):
        x_copy(zero, dx).wait_send()

    @pl.when(core == 0)
    def _():
        for way in range(2):
            for hop in range(4):
                ring_copy(way, hop).wait_send()

    @pl.when(core == 1)
    def _():
        for dz in range(1, 8):
            vz_copy(dz).wait_send()
        for g in range(1, GROUPS):
            for dx in range(1, 4):
                x_copy(jnp.int32(g), dx).wait_send()

    for g in range(GROUPS):
        core_copy(jnp.int32(g)).wait_send()
    pair_q.wait_send()
    pair_o.wait_send()
    pair_s.wait_send()


def body(queries, key_rows, value_rows, document_lengths):
    sems = pltpu.SemaphoreType.DMA
    vmem = pl.BlockSpec(memory_space=pltpu.VMEM)
    attended = pl.pallas_call(
        kernel,
        out_shape=jax.ShapeDtypeStruct((ROWS, HEADS * 128), jnp.bfloat16),
        in_specs=[pl.BlockSpec(memory_space=pltpu.SMEM), vmem, vmem, vmem],
        out_specs=vmem,
        scratch_shapes=[
            pltpu.VMEM((2, GROUPS, 2, 512, 128), jnp.bfloat16),
            pltpu.VMEM((GROUPS, 2, 512, 128), jnp.bfloat16),
            pltpu.VMEM((2, WIDE, 256), jnp.bfloat16),
            pltpu.VMEM((ROWS, HEADS * 128), jnp.bfloat16),
            pltpu.VMEM((KEYS, WIDE), jnp.float32),
            pltpu.VMEM((KEYS, WIDE), jnp.float32),
            pltpu.VMEM((2, 128, WIDE), jnp.float32),
            pltpu.VMEM((2, 1, WIDE), jnp.float32),
            pltpu.VMEM((2, 1, WIDE), jnp.float32),
            pltpu.VMEM((1, WIDE), jnp.float32),
            pltpu.VMEM((1, WIDE), jnp.float32),
            pltpu.VMEM((128, WIDE), jnp.bfloat16),
            pltpu.VMEM((128, WIDE), jnp.bfloat16),
            pltpu.VMEM((8, WIDE), jnp.float32),
            pltpu.VMEM((8, WIDE), jnp.float32),
            sems((2, 2)), sems((4,)), sems((GROUPS, 4)), sems((GROUPS, 4)), sems((8,)), sems((8,)),
            sems((4,)), sems((4,)), sems((4,)), sems((4,)),
            sems((GROUPS,)), sems((GROUPS,)), sems((3,)), sems((3,)),
        ],
        compiler_params=pltpu.CompilerParams(
            collective_id=0, has_side_effects=True, vmem_limit_bytes=48 * 2**20
        ),
        cost_estimate=pl.CostEstimate(flops=2 * 2 * 9216 * WIDE * 128, bytes_accessed=2**20, transcendentals=9216 * WIDE),
    )(document_lengths, queries[0], key_rows[0], value_rows[0])
    return attended[None]


def solution(mesh):
    in_specs = (
        P(None, "ctx", "head"),
        P(None, ("ctx", "head"), None),
        P(None, ("ctx", "head"), None),
        P(),
    )
    out_specs = P(None, "ctx", "head")
    return jax.shard_map(body, mesh=mesh, in_specs=in_specs, out_specs=out_specs, check_vma=False)
```

```python
import functools
import math

import jax
import jax.numpy as jnp
from jax import lax
from jax.experimental import pallas as pl
from jax.experimental.pallas import tpu as pltpu
from jax.sharding import PartitionSpec as P

MESH = pl.DeviceIdType.MESH
HIDE = -(2.0**100)
SCALE = math.log2(math.e) / math.sqrt(128.0)
ROWS = 256
HEADS = 4
WIDE = ROWS * HEADS
KEYS = 256
GROUPS = 8
STEPS = 2 * GROUPS
ORDERS = (
    (0, 8, 9, 10, 11, 12, 13, 14, 15, 1, 2, 3, 4, 5, 6, 7),
    (0, 8, 9, 1, 10, 2, 11, 12, 3, 13, 14, 15, 4, 5, 6, 7),
)
FIRST = ((0, (1, 3, 2, 0)), (1, (0, 1, 7, 2, 6, 3, 5, 4)))
LAST = ()


def device_at(y, x, z, core):
    return ((y % 2) * 32 + x * 8 + z, (y // 2) * 2 + core)


def kernel(
    lengths, q_ref, k_ref, v_ref, o_ref,
    kv, dk, qa, q1, q2, score_a, score_b, acc, top, total, best_a, best_b, o_out, o_in, s_out, s_in,
    k_send, k_recv, v_send, v_recv, x_send, x_recv, r_send, r_recv, l_send, l_recv,
    core_send, core_recv, pair_send, pair_recv, q_sem,
):
    ctx = lax.axis_index("ctx")
    head = lax.axis_index("head")
    y_lo, x, z = ctx // 32, (ctx // 8) % 4, ctx % 8
    y_hi, core = head // 2, head % 2
    y = y_hi * 2 + y_lo
    sibling = device_at(y, x, z, 1 - core)
    partner_y = (y + 4 + (1 - 2 * y_lo) * (1 - 2 * core)) % 4
    partner = device_at(partner_y, 3 - x, z, core)

    q_load = pltpu.make_async_copy(q_ref, q1, q_sem)
    q_load.start()

    barrier = pltpu.get_barrier_semaphore()

    def greet(y_of, x_of, z_of, core_of):
        pl.semaphore_signal(barrier, inc=1, device_id=device_at(y_of, x_of, z_of, core_of), device_id_type=MESH)

    @pl.when(core == 0)
    def _():
        for yy in range(4):
            for dx in range(4):
                if dx == 0:
                    pl.when((yy != y) | (y_lo != core))(lambda yy=yy: greet(jnp.int32(yy), x, z, y_lo))
                else:
                    greet(jnp.int32(yy), (x + dx) % 4, z, y_lo)
        for dz in (1, 7):
            greet(y, x, (z + dz) % 8, core)

    @pl.when(core == 1)
    def _():
        for yy in range(4):
            for dz in range(8):
                if dz == 0:
                    pl.when((yy != y) | (y_lo != core))(lambda yy=yy: greet(jnp.int32(yy), x, z, y_lo))
                else:
                    greet(jnp.int32(yy), x, (z + dz) % 8, y_lo)
        for dx in range(1, 4):
            greet(y, (x + dx) % 4, z, core)

    greet(y, x, z, 1 - core)
    greet(partner_y, 3 - x, z, core)

    starts, ends, run = [], [], jnp.int32(0)
    for d in range(4):
        starts.append(run)
        run = run + lengths[0, d]
        ends.append(run)

    def fill_queries(which, source):
        late = jnp.where(which == 0, y_lo, 1 - y_lo)
        own_x = jnp.where(which == 0, x, 3 - x)
        block = late * 32 + own_x * 8 + z
        pos = block * ROWS + lax.broadcasted_iota(jnp.int32, (ROWS, 128), 0)
        lane = lax.broadcasted_iota(jnp.int32, (ROWS, 128), 1)
        hide = lane - 64 > block
        for d in range(4):
            inside = (pos >= starts[d]) & (pos < ends[d])
            hide = hide | ((lane == d) & jnp.logical_not(inside))
        extra = jnp.where(hide, HIDE, 0.0).astype(jnp.bfloat16)
        for h in range(HEADS):
            qa[which, h * ROWS : (h + 1) * ROWS, 0:128] = source[:, h * 128 : (h + 1) * 128]
            qa[which, h * ROWS : (h + 1) * ROWS, 128:256] = extra

    def fill_keys(index, carry):
        group, late = index // 2, index % 2
        row = lax.broadcasted_iota(jnp.int32, (512, 128), 0)
        lane = lax.broadcasted_iota(jnp.int32, (512, 128), 1)
        block = late * 32 + (row // 128) * 8 + group
        pos = block * ROWS + ((row // 64) % 2) * 128 + y_lo * 64 + row % 64
        show = lane - 64 == block
        for d in range(4):
            show = show | ((lane == d) & (pos >= starts[d]) & (pos < ends[d]))
        dk[group, late] = jnp.where(show, 1.0, 0.0).astype(jnp.bfloat16)
        return carry

    lax.fori_loop(0, 2 * GROUPS, fill_keys, 0)
    acc[...] = jnp.zeros_like(acc)
    total[...] = jnp.zeros_like(total)
    top[...] = jnp.full_like(top, -1e38)
    pl.semaphore_wait(barrier, 28 + core - jnp.where(y_lo == core, 1, 0))

    def own_copy(kind, turn, step):
        rows = kv.at[kind, z, y_lo, pl.ds(x * 128 + y_hi * 64, 64), :]
        if kind == 0:
            target = device_at(core + 2 * turn, (x + step) % 4, z, 0)
            send, recv = k_send.at[turn, step], k_recv.at[0]
        else:
            target = device_at(core + 2 * turn, x, (z + step) % 8, 1)
            send, recv = v_send.at[turn, step], v_recv.at[step]
        return pltpu.make_async_remote_copy(
            src_ref=(k_ref, v_ref)[kind], dst_ref=rows, send_sem=send, recv_sem=recv,
            device_id=target, device_id_type=MESH,
        )

    def own_stay(kind):
        rows = kv.at[kind, z, y_lo, pl.ds(x * 128 + y_hi * 64, 64), :]
        return pltpu.make_async_copy((k_ref, v_ref)[kind], rows, (k_recv, v_recv)[kind].at[0])

    def own_each(act, stay, orders):
        for kind, order in orders:
            for step in order:
                for turn in range(2):
                    if step:
                        act(kind, turn, step)
                    else:
                        here = (core + 2 * turn == y) & (core == kind)
                        pl.when(here)(lambda kind=kind: stay(kind))
                        pl.when(jnp.logical_not(here))(lambda kind=kind, turn=turn: act(kind, turn, 0))

    own_each(lambda *a: own_copy(*a).start(), lambda kind: own_stay(kind).start(), FIRST)

    pair_q = pltpu.make_async_remote_copy(
        src_ref=q_ref, dst_ref=q2, send_sem=pair_send.at[0], recv_sem=pair_recv.at[0],
        device_id=partner, device_id_type=MESH,
    )
    pair_o = pltpu.make_async_remote_copy(
        src_ref=o_out, dst_ref=o_in, send_sem=pair_send.at[1], recv_sem=pair_recv.at[1],
        device_id=partner, device_id_type=MESH,
    )
    pair_s = pltpu.make_async_remote_copy(
        src_ref=s_out, dst_ref=s_in, send_sem=pair_send.at[2], recv_sem=pair_recv.at[2],
        device_id=partner, device_id_type=MESH,
    )

    def z_of(g):
        far = (g + 1) // 2
        return (z + 8 + jnp.where(g % 2 == 1, -far, far)) % 8

    def column(at_x, at_z):
        return kv.at[core, at_z, :, pl.ds(at_x * 128, 128), :]

    def x_copy(g, dx):
        part = column(x, z_of(g))
        return pltpu.make_async_remote_copy(
            src_ref=part, dst_ref=part, send_sem=x_send.at[g, dx], recv_sem=x_recv.at[g, dx],
            device_id=device_at(y, (x + dx) % 4, z, core), device_id_type=MESH,
        )

    def x_wait(g, dx):
        part = column((x + 4 - dx) % 4, z_of(g))
        pltpu.make_async_copy(part, part, x_recv.at[g, dx]).wait()

    def ring_copy(way, hop, part):
        at = (z + 8 + jnp.where(way == 0, -hop, hop)) % 8
        half = kv.at[0, at, part]
        send, recv = ((r_send, r_recv), (l_send, l_recv))[way]
        return pltpu.make_async_remote_copy(
            src_ref=half, dst_ref=half, send_sem=send.at[hop, part], recv_sem=recv.at[hop, part],
            device_id=device_at(y, x, (z + (1, 7)[way]) % 8, core), device_id_type=MESH,
        )

    def ring_wait(way, hop, part):
        at = (z + 8 + jnp.where(way == 0, -hop - 1, hop + 1)) % 8
        half = kv.at[0, at, part]
        pltpu.make_async_copy(half, half, (r_recv, l_recv)[way].at[hop, part]).wait()

    def core_copy(g):
        part = kv.at[core, z_of(g)]
        return pltpu.make_async_remote_copy(
            src_ref=part, dst_ref=part, send_sem=core_send.at[g], recv_sem=core_recv.at[g],
            device_id=sibling, device_id_type=MESH,
        )

    def core_wait(g):
        part = kv.at[1 - core, z_of(g)]
        pltpu.make_async_copy(part, part, core_recv.at[g]).wait()

    def relay_values(g):
        dz = (z + 8 - z_of(g)) % 8
        part = column(x, z_of(g))
        pltpu.make_async_copy(part, part, v_recv.at[dz]).wait()
        for dx in range(1, 4):
            x_copy(g, dx).start()

    def relay(groups):
        @pl.when(core == 1)
        def _():
            for g in groups:
                relay_values(jnp.int32(g))

    def fetch(g):
        for hop in range(4):

            @pl.when((core == 0) & (g == 2 * hop + 1))
            def _():
                for part in range(2):
                    for way in range(2):
                        if hop < 3:
                            ring_wait(way, hop, part)
                        elif way == part:
                            ring_wait(way, hop, part)
                        if hop < 2 or (hop == 2 and way == part):
                            ring_copy(way, hop + 1, part).start()
                core_copy(g).start()
                if hop < 3:
                    core_copy(g + 1).start()

        @pl.when(core == 1)
        def _():
            for dx in range(1, 4):
                x_wait(g, dx)
            core_copy(g).start()

        pl.when(g == 1)(lambda: relay((3, 4)))
        pl.when(g == 2)(lambda: relay((5, 6)))
        pl.when(g == 3)(lambda: relay((7,)))

    zero = jnp.int32(0)
    pair_q.start()
    q_load.wait()
    fill_queries(0, q1)

    @pl.when(core == 0)
    def _():
        whole = kv.at[0, z]
        pltpu.make_async_copy(whole, whole, k_recv.at[0]).wait()
        for part in range(2):
            for way in range(2):
                ring_copy(way, 0, part).start()

    relay((0, 1, 2))
    own_each(lambda *a: own_copy(*a).start(), lambda kind: own_stay(kind).start(), LAST)

    @pl.when(core == 1)
    def _():
        for dx in range(1, 4):
            x_wait(zero, dx)

    core_copy(zero).start()

    def step_of(i):
        code = jnp.int32(ORDERS[1][0])
        for n in range(STEPS):
            code = jnp.where(i == n, jnp.where(y_lo == 0, ORDERS[0][n], ORDERS[1][n]), code)
        return code // GROUPS, code % GROUPS

    def units_of(which, g):
        late = jnp.where(which == 0, y_lo, 1 - y_lo)
        own_x = jnp.where(which == 0, x, 3 - x)
        blocks = own_x + jnp.where(z_of(g) <= z, 1, 0)
        count = (blocks + 1) // 2
        return jnp.where(late == 1, 2 + count, jnp.maximum(count, 1))

    def locate(i, j):
        which, g = step_of(i)
        over = i >= STEPS
        which = jnp.where(over, y_lo, which)
        group = jnp.where(over, z, z_of(g))
        late = jnp.where(over, 1, j // 2)
        row = pl.multiple_of(jnp.where(over, 0, (j % 2) * KEYS), KEYS)
        return which, group, late, row

    def advance(i, j):
        which, g = step_of(i)
        more = (j + 1 < units_of(which, g)) & (i < STEPS)
        return jnp.where(more, i, jnp.minimum(i + 1, STEPS)), jnp.where(more, j + 1, 0)

    def prepare(i, j, got):
        which, g = step_of(i)
        first = (j == 0) & (i < STEPS)
        fresh = first & (g == got)
        pl.when(fresh)(lambda: core_wait(g))
        got = jnp.where(fresh, got + 1, got)

        @pl.when(first & (which == 1) & (g == 0))
        def _():
            pair_q.wait_recv()
            fill_queries(1, q2)

        last = (j == 0) & (i + 1 < STEPS)
        pl.when(last & (step_of(i + 1)[1] == got))(lambda: fetch(got))
        return got

    def scores_of(i, j, score, best):
        which, group, late, row = locate(i, j)
        keys = jnp.concatenate([kv[0, group, late, pl.ds(row, KEYS), :], dk[group, late, pl.ds(row, KEYS), :]], axis=1)
        s = lax.dot_general(keys, qa[which], (((1,), (1,)), ((), ())), preferred_element_type=jnp.float32)
        score[...] = s
        best[...] = jnp.max(s, axis=0, keepdims=True)

    def diagonal(i, j, score, best):
        which, g = step_of(i)

        @pl.when((i < STEPS) & (g == 0) & (j + 1 == units_of(which, g)))
        def _():
            late = jnp.where(which == 0, y_lo, 1 - y_lo)
            own_x = jnp.where(which == 0, x, 3 - x)
            row = lax.broadcasted_iota(jnp.int32, (KEYS, WIDE), 0) + (j % 2) * KEYS
            key_pos = ((j // 2) * 32 + (row // 128) * 8 + z) * ROWS + ((row // 64) % 2) * 128 + y_lo * 64 + row % 64
            query_pos = (late * 32 + own_x * 8 + z) * ROWS + lax.broadcasted_iota(jnp.int32, (KEYS, WIDE), 1) % ROWS
            s = jnp.where(key_pos <= query_pos, score[...], HIDE)
            score[...] = s
            best[...] = jnp.max(s, axis=0, keepdims=True)

    def soften(i, j, score, best):
        which, group, late, row = locate(i, j)
        old = top[which]
        new = jnp.maximum(old, best[...])
        weights = jnp.exp2((score[...] - new) * SCALE)
        factor = jnp.exp2((old - new) * SCALE)
        top[which] = new
        total[which] = total[which] * factor + jnp.sum(weights, axis=0, keepdims=True)
        values = kv[1, group, late, pl.ds(row, KEYS), :]
        mixed = lax.dot_general(
            values, weights.astype(jnp.bfloat16), (((0,), (0,)), ((), ())), preferred_element_type=jnp.float32
        )
        acc[which] = acc[which] * factor + mixed

    def hand_back(i, j):
        which, g = step_of(i)

        @pl.when((i < STEPS) & (which == 1) & (g == GROUPS - 1) & (j + 1 == units_of(which, g)))
        def _():
            o_out[...] = (acc[1] / total[1]).astype(jnp.bfloat16)
            s_out[0:1, :] = top[1]
            s_out[1:2, :] = total[1]
            pair_o.start()
            pair_s.start()

    def two_units(turn, state):
        i, j, got = state
        i_b, j_b = advance(i, j)
        got = prepare(i_b, j_b, got)
        scores_of(i_b, j_b, score_b, best_b)
        soften(i, j, score_a, best_a)
        diagonal(i_b, j_b, score_b, best_b)
        hand_back(i, j)
        i_c, j_c = advance(i_b, j_b)
        got = prepare(i_c, j_c, got)
        scores_of(i_c, j_c, score_a, best_a)
        soften(i_b, j_b, score_b, best_b)
        diagonal(i_c, j_c, score_a, best_a)
        hand_back(i_b, j_b)
        return i_c, j_c, got

    units = jnp.int32(0)
    for which in range(2):
        for g in range(GROUPS):
            units = units + units_of(jnp.int32(which), jnp.int32(g))
    got = prepare(zero, zero, zero)
    scores_of(zero, zero, score_a, best_a)
    diagonal(zero, zero, score_a, best_a)
    lax.fori_loop(0, (units + 1) // 2, two_units, (zero, zero, got))

    pair_o.wait_recv()
    pair_s.wait_recv()
    peak = jnp.maximum(top[0], s_in[0:1, :])
    mine = jnp.exp2((top[0] - peak) * SCALE)
    other = jnp.exp2((s_in[0:1, :] - peak) * SCALE) * s_in[1:2, :]
    whole = mine * total[0] + other
    mine, other = mine / whole, other / whole
    for h in range(HEADS):
        part = slice(h * ROWS, (h + 1) * ROWS)
        merged = acc[0, :, part] * mine[:, part] + o_in[:, part].astype(jnp.float32) * other[:, part]
        o_ref[:, h * 128 : (h + 1) * 128] = merged.T.astype(jnp.bfloat16)

    own_each(lambda *a: own_copy(*a).wait_send(), lambda kind: None, FIRST + LAST)

    @pl.when(core == 0)
    def _():
        for way in range(2):
            for hop in range(4):
                for part in range(2):
                    if hop < 3 or part == way:
                        ring_copy(way, hop, part).wait_send()

    @pl.when(core == 1)
    def _():
        for g in range(GROUPS):
            for dx in range(1, 4):
                x_copy(jnp.int32(g), dx).wait_send()

    for g in range(GROUPS):
        core_copy(jnp.int32(g)).wait_send()
    pair_q.wait_send()
    pair_o.wait_send()
    pair_s.wait_send()


def body(queries, key_rows, value_rows, document_lengths):
    sems = pltpu.SemaphoreType.DMA
    vmem = pl.BlockSpec(memory_space=pltpu.VMEM)
    attended = pl.pallas_call(
        kernel,
        out_shape=jax.ShapeDtypeStruct((ROWS, HEADS * 128), jnp.bfloat16),
        in_specs=[pl.BlockSpec(memory_space=pltpu.SMEM)] + [pl.BlockSpec(memory_space=pl.ANY)] * 3,
        out_specs=vmem,
        scratch_shapes=[
            pltpu.VMEM((2, GROUPS, 2, 512, 128), jnp.bfloat16),
            pltpu.VMEM((GROUPS, 2, 512, 128), jnp.bfloat16),
            pltpu.VMEM((2, WIDE, 256), jnp.bfloat16),
            pltpu.VMEM((ROWS, HEADS * 128), jnp.bfloat16),
            pltpu.VMEM((ROWS, HEADS * 128), jnp.bfloat16),
            pltpu.VMEM((KEYS, WIDE), jnp.float32),
            pltpu.VMEM((KEYS, WIDE), jnp.float32),
            pltpu.VMEM((2, 128, WIDE), jnp.float32),
            pltpu.VMEM((2, 1, WIDE), jnp.float32),
            pltpu.VMEM((2, 1, WIDE), jnp.float32),
            pltpu.VMEM((1, WIDE), jnp.float32),
            pltpu.VMEM((1, WIDE), jnp.float32),
            pltpu.VMEM((128, WIDE), jnp.bfloat16),
            pltpu.VMEM((128, WIDE), jnp.bfloat16),
            pltpu.VMEM((8, WIDE), jnp.float32),
            pltpu.VMEM((8, WIDE), jnp.float32),
            sems((2, 4)), sems((1,)), sems((2, 8)), sems((8,)), sems((GROUPS, 4)), sems((GROUPS, 4)),
            sems((4, 2)), sems((4, 2)), sems((4, 2)), sems((4, 2)),
            sems((GROUPS,)), sems((GROUPS,)), sems((3,)), sems((3,)), sems,
        ],
        compiler_params=pltpu.CompilerParams(
            collective_id=0, has_side_effects=True, vmem_limit_bytes=63 * 2**20
        ),
        cost_estimate=pl.CostEstimate(flops=2 * 2 * 9216 * WIDE * 128, bytes_accessed=2**20, transcendentals=9216 * WIDE),
    )(document_lengths, queries[0], key_rows[0], value_rows[0])
    return attended[None]


def solution(mesh):
    in_specs = (
        P(None, "ctx", "head"),
        P(None, ("ctx", "head"), None),
        P(None, ("ctx", "head"), None),
        P(),
    )
    out_specs = P(None, "ctx", "head")
    return jax.shard_map(body, mesh=mesh, in_specs=in_specs, out_specs=out_specs, check_vma=False)
```

```python
import functools
import math

import jax
import jax.numpy as jnp
from jax import lax
from jax.experimental import pallas as pl
from jax.experimental.pallas import tpu as pltpu
from jax.sharding import PartitionSpec as P

MESH = pl.DeviceIdType.MESH
HIDE = -(2.0**100)
SCALE = math.log2(math.e) / math.sqrt(128.0)
ROWS = 256
HEADS = 4
WIDE = ROWS * HEADS
KEYS = 256
GROUPS = 8
STEPS = 2 * GROUPS
ORDERS = (
    (0, 8, 9, 10, 11, 12, 13, 14, 15, 1, 2, 3, 4, 5, 6, 7),
    (0, 8, 9, 1, 10, 2, 11, 12, 3, 13, 14, 15, 4, 5, 6, 7),
)
RELAY_AT = 2
FIRST = ((0, (1, 3, 2, 0)), (1, (0, 1, 7, 2, 6, 3, 5, 4)))
LAST = ()


def device_at(y, x, z, core):
    return ((y % 2) * 32 + x * 8 + z, (y // 2) * 2 + core)


def kernel(
    lengths, q_ref, k_ref, v_ref, o_ref,
    kv, dk, qa, q1, q2, score_a, score_b, acc, top, total, best_a, best_b, o_out, o_in, s_out, s_in,
    k_send, k_recv, v_send, v_recv, x_send, x_recv, r_send, r_recv, l_send, l_recv,
    core_send, core_recv, pair_send, pair_recv, q_sem,
):
    ctx = lax.axis_index("ctx")
    head = lax.axis_index("head")
    y_lo, x, z = ctx // 32, (ctx // 8) % 4, ctx % 8
    y_hi, core = head // 2, head % 2
    y = y_hi * 2 + y_lo
    sibling = device_at(y, x, z, 1 - core)
    partner_y = (y + 4 + (1 - 2 * y_lo) * (1 - 2 * core)) % 4
    partner = device_at(partner_y, 3 - x, z, core)

    q_load = pltpu.make_async_copy(q_ref, q1, q_sem)
    q_load.start()

    barrier = pltpu.get_barrier_semaphore()

    def greet(y_of, x_of, z_of, core_of):
        pl.semaphore_signal(barrier, inc=1, device_id=device_at(y_of, x_of, z_of, core_of), device_id_type=MESH)

    @pl.when(core == 0)
    def _():
        for yy in range(4):
            for dx in range(4):
                if dx == 0:
                    pl.when((yy != y) | (y_lo != core))(lambda yy=yy: greet(jnp.int32(yy), x, z, y_lo))
                else:
                    greet(jnp.int32(yy), (x + dx) % 4, z, y_lo)
        for dz in (1, 2, 6, 7):
            greet(y, x, (z + dz) % 8, core)

    @pl.when(core == 1)
    def _():
        for yy in range(4):
            for dz in range(8):
                if dz == 0:
                    pl.when((yy != y) | (y_lo != core))(lambda yy=yy: greet(jnp.int32(yy), x, z, y_lo))
                else:
                    greet(jnp.int32(yy), x, (z + dz) % 8, y_lo)
        for dx in range(1, 4):
            greet(y, (x + dx) % 4, z, core)

    greet(y, x, z, 1 - core)
    greet(partner_y, 3 - x, z, core)

    starts, ends, run = [], [], jnp.int32(0)
    for d in range(4):
        starts.append(run)
        run = run + lengths[0, d]
        ends.append(run)

    def fill_queries(which, source):
        late = jnp.where(which == 0, y_lo, 1 - y_lo)
        own_x = jnp.where(which == 0, x, 3 - x)
        block = late * 32 + own_x * 8 + z
        pos = block * ROWS + lax.broadcasted_iota(jnp.int32, (ROWS, 128), 0)
        lane = lax.broadcasted_iota(jnp.int32, (ROWS, 128), 1)
        hide = lane - 64 > block
        for d in range(4):
            inside = (pos >= starts[d]) & (pos < ends[d])
            hide = hide | ((lane == d) & jnp.logical_not(inside))
        extra = jnp.where(hide, HIDE, 0.0).astype(jnp.bfloat16)
        for h in range(HEADS):
            qa[which, h * ROWS : (h + 1) * ROWS, 0:128] = source[:, h * 128 : (h + 1) * 128]
            qa[which, h * ROWS : (h + 1) * ROWS, 128:256] = extra

    def fill_keys(index, carry):
        group, late = index // 2, index % 2
        row = lax.broadcasted_iota(jnp.int32, (512, 128), 0)
        lane = lax.broadcasted_iota(jnp.int32, (512, 128), 1)
        block = late * 32 + (row // 128) * 8 + group
        pos = block * ROWS + ((row // 64) % 2) * 128 + y_lo * 64 + row % 64
        show = lane - 64 == block
        for d in range(4):
            show = show | ((lane == d) & (pos >= starts[d]) & (pos < ends[d]))
        dk[group, late] = jnp.where(show, 1.0, 0.0).astype(jnp.bfloat16)
        return carry

    lax.fori_loop(0, 2 * GROUPS, fill_keys, 0)
    acc[...] = jnp.zeros_like(acc)
    total[...] = jnp.zeros_like(total)
    top[...] = jnp.full_like(top, -1e38)
    pl.semaphore_wait(barrier, 30 - core - jnp.where(y_lo == core, 1, 0))

    def own_copy(kind, turn, step):
        rows = kv.at[kind, z, y_lo, pl.ds(x * 128 + y_hi * 64, 64), :]
        if kind == 0:
            target = device_at(core + 2 * turn, (x + step) % 4, z, 0)
            send, recv = k_send.at[turn, step], k_recv.at[0]
        else:
            target = device_at(core + 2 * turn, x, (z + step) % 8, 1)
            send, recv = v_send.at[turn, step], v_recv.at[step]
        return pltpu.make_async_remote_copy(
            src_ref=(k_ref, v_ref)[kind], dst_ref=rows, send_sem=send, recv_sem=recv,
            device_id=target, device_id_type=MESH,
        )

    def own_stay(kind):
        rows = kv.at[kind, z, y_lo, pl.ds(x * 128 + y_hi * 64, 64), :]
        return pltpu.make_async_copy((k_ref, v_ref)[kind], rows, (k_recv, v_recv)[kind].at[0])

    def own_each(act, stay, orders):
        for kind, order in orders:
            for step in order:
                for turn in range(2):
                    if step:
                        act(kind, turn, step)
                    else:
                        here = (core + 2 * turn == y) & (core == kind)
                        pl.when(here)(lambda kind=kind: stay(kind))
                        pl.when(jnp.logical_not(here))(lambda kind=kind, turn=turn: act(kind, turn, 0))

    own_each(lambda *a: own_copy(*a).start(), lambda kind: own_stay(kind).start(), FIRST)

    pair_q = pltpu.make_async_remote_copy(
        src_ref=q_ref, dst_ref=q2, send_sem=pair_send.at[0], recv_sem=pair_recv.at[0],
        device_id=partner, device_id_type=MESH,
    )
    pair_o = pltpu.make_async_remote_copy(
        src_ref=o_out, dst_ref=o_in, send_sem=pair_send.at[1], recv_sem=pair_recv.at[1],
        device_id=partner, device_id_type=MESH,
    )
    pair_s = pltpu.make_async_remote_copy(
        src_ref=s_out, dst_ref=s_in, send_sem=pair_send.at[2], recv_sem=pair_recv.at[2],
        device_id=partner, device_id_type=MESH,
    )

    def z_of(g):
        far = (g + 1) // 2
        return (z + 8 + jnp.where(g % 2 == 1, -far, far)) % 8

    def column(at_x, at_z):
        return kv.at[core, at_z, :, pl.ds(at_x * 128, 128), :]

    def x_copy(g, dx):
        part = column(x, z_of(g))
        return pltpu.make_async_remote_copy(
            src_ref=part, dst_ref=part, send_sem=x_send.at[g, dx], recv_sem=x_recv.at[g, dx],
            device_id=device_at(y, (x + dx) % 4, z, core), device_id_type=MESH,
        )

    def x_wait(g, dx):
        part = column((x + 4 - dx) % 4, z_of(g))
        pltpu.make_async_copy(part, part, x_recv.at[g, dx]).wait()

    def ring_copy(way, hop, part):
        back = 0 if hop < 2 else 2
        far = 1 + hop % 2
        at = (z + 8 + jnp.where(way == 0, -back, back)) % 8
        half = kv.at[0, at, part]
        send, recv = ((r_send, r_recv), (l_send, l_recv))[way]
        return pltpu.make_async_remote_copy(
            src_ref=half, dst_ref=half, send_sem=send.at[hop, part], recv_sem=recv.at[hop, part],
            device_id=device_at(y, x, (z + (far, 8 - far)[way]) % 8, core), device_id_type=MESH,
        )

    def ring_wait(way, hop, part):
        at = (z + 8 + jnp.where(way == 0, -hop - 1, hop + 1)) % 8
        half = kv.at[0, at, part]
        pltpu.make_async_copy(half, half, (r_recv, l_recv)[way].at[hop, part]).wait()

    def core_copy(g):
        part = kv.at[core, z_of(g)]
        return pltpu.make_async_remote_copy(
            src_ref=part, dst_ref=part, send_sem=core_send.at[g], recv_sem=core_recv.at[g],
            device_id=sibling, device_id_type=MESH,
        )

    def core_wait(g):
        part = kv.at[1 - core, z_of(g)]
        pltpu.make_async_copy(part, part, core_recv.at[g]).wait()

    def relay_values(g):
        dz = (z + 8 - z_of(g)) % 8
        part = column(x, z_of(g))
        pltpu.make_async_copy(part, part, v_recv.at[dz]).wait()
        for dx in range(1, 4):
            x_copy(g, dx).start()

    def relay(groups):
        @pl.when(core == 1)
        def _():
            for g in groups:
                relay_values(jnp.int32(g))

    def fetch(g):
        for hop in range(4):

            @pl.when((core == 0) & (g == 2 * hop + 1))
            def _():
                for part in range(2):
                    for way in range(2):
                        if hop % 2 == 0 or (hop == 3 and way == part):
                            ring_wait(way, hop, part)
                core_copy(g).start()
                if hop < 3:
                    core_copy(g + 1).start()

        @pl.when(core == 1)
        def _():
            for dx in range(1, 4):
                x_wait(g, dx)
            core_copy(g).start()

        @pl.when((core == 0) & (g == RELAY_AT))
        def _():
            for part in range(2):
                for way in range(2):
                    ring_wait(way, 1, part)
                    ring_copy(way, 2, part).start()
            for way in range(2):
                ring_copy(way, 3, way).start()

        pl.when(g == 1)(lambda: relay((3, 4)))
        pl.when(g == 2)(lambda: relay((5, 6)))
        pl.when(g == 3)(lambda: relay((7,)))

    zero = jnp.int32(0)
    pair_q.start()
    q_load.wait()
    fill_queries(0, q1)

    @pl.when(core == 0)
    def _():
        whole = kv.at[0, z]
        pltpu.make_async_copy(whole, whole, k_recv.at[0]).wait()
        for hop in range(2):
            for part in range(2):
                for way in range(2):
                    ring_copy(way, hop, part).start()

    relay((0, 1, 2))
    @pl.when(core == 1)
    def _():
        for dx in range(1, 4):
            x_wait(zero, dx)

    core_copy(zero).start()
    own_each(lambda *a: own_copy(*a).start(), lambda kind: own_stay(kind).start(), LAST)

    def step_of(i):
        code = jnp.int32(ORDERS[1][0])
        for n in range(STEPS):
            code = jnp.where(i == n, jnp.where(y_lo == 0, ORDERS[0][n], ORDERS[1][n]), code)
        return code // GROUPS, code % GROUPS

    def units_of(which, g):
        late = jnp.where(which == 0, y_lo, 1 - y_lo)
        own_x = jnp.where(which == 0, x, 3 - x)
        blocks = own_x + jnp.where(z_of(g) <= z, 1, 0)
        count = (blocks + 1) // 2
        return jnp.where(late == 1, 2 + count, jnp.maximum(count, 1))

    def locate(i, j):
        which, g = step_of(i)
        over = i >= STEPS
        which = jnp.where(over, y_lo, which)
        group = jnp.where(over, z, z_of(g))
        late = jnp.where(over, 1, j // 2)
        row = pl.multiple_of(jnp.where(over, 0, (j % 2) * KEYS), KEYS)
        return which, group, late, row

    def advance(i, j):
        which, g = step_of(i)
        more = (j + 1 < units_of(which, g)) & (i < STEPS)
        return jnp.where(more, i, jnp.minimum(i + 1, STEPS)), jnp.where(more, j + 1, 0)

    def touches_first(i):
        answer = jnp.bool_(False)
        for parity, order in enumerate(ORDERS):
            for n in range(STEPS):
                if order[n] % GROUPS not in [code % GROUPS for code in order[:n]]:
                    answer = answer | ((i == n) & (y_lo == parity))
        return answer

    def prepare(i, j, got):
        which, g = step_of(i)
        first = (j == 0) & (i < STEPS)
        pl.when(first & touches_first(i))(lambda: core_wait(g))

        @pl.when(first & (which == 1) & (g == 0))
        def _():
            pair_q.wait_recv()
            fill_queries(1, q2)

        last = j + 1 == units_of(which, g)
        soon = (first & (i + 1 < STEPS) & (step_of(i + 1)[1] == got)) | (
            last & (i + 2 < STEPS) & (step_of(i + 2)[1] == got)
        )
        pl.when(soon)(lambda: fetch(got))
        return jnp.where(soon, got + 1, got)

    def scores_of(i, j, score, best):
        which, group, late, row = locate(i, j)
        keys = jnp.concatenate([kv[0, group, late, pl.ds(row, KEYS), :], dk[group, late, pl.ds(row, KEYS), :]], axis=1)
        s = lax.dot_general(keys, qa[which], (((1,), (1,)), ((), ())), preferred_element_type=jnp.float32)
        score[...] = s
        best[...] = jnp.max(s, axis=0, keepdims=True)

    def diagonal(i, j, score, best):
        which, g = step_of(i)

        @pl.when((i < STEPS) & (g == 0) & (j + 1 == units_of(which, g)))
        def _():
            late = jnp.where(which == 0, y_lo, 1 - y_lo)
            own_x = jnp.where(which == 0, x, 3 - x)
            row = lax.broadcasted_iota(jnp.int32, (KEYS, WIDE), 0) + (j % 2) * KEYS
            key_pos = ((j // 2) * 32 + (row // 128) * 8 + z) * ROWS + ((row // 64) % 2) * 128 + y_lo * 64 + row % 64
            query_pos = (late * 32 + own_x * 8 + z) * ROWS + lax.broadcasted_iota(jnp.int32, (KEYS, WIDE), 1) % ROWS
            s = jnp.where(key_pos <= query_pos, score[...], HIDE)
            score[...] = s
            best[...] = jnp.max(s, axis=0, keepdims=True)

    def soften(i, j, score, best):
        which, group, late, row = locate(i, j)
        old = top[which]
        new = jnp.maximum(old, best[...])
        weights = jnp.exp2((score[...] - new) * SCALE)
        factor = jnp.exp2((old - new) * SCALE)
        top[which] = new
        total[which] = total[which] * factor + jnp.sum(weights, axis=0, keepdims=True)
        values = kv[1, group, late, pl.ds(row, KEYS), :]
        mixed = lax.dot_general(
            values, weights.astype(jnp.bfloat16), (((0,), (0,)), ((), ())), preferred_element_type=jnp.float32
        )
        acc[which] = acc[which] * factor + mixed

    def hand_back(i, j):
        which, g = step_of(i)

        @pl.when((i < STEPS) & (which == 1) & (g == GROUPS - 1) & (j + 1 == units_of(which, g)))
        def _():
            o_out[...] = (acc[1] / total[1]).astype(jnp.bfloat16)
            s_out[0:1, :] = top[1]
            s_out[1:2, :] = total[1]
            pair_o.start()
            pair_s.start()

    def two_units(turn, state):
        i, j, got = state
        i_b, j_b = advance(i, j)
        got = prepare(i_b, j_b, got)
        scores_of(i_b, j_b, score_b, best_b)
        soften(i, j, score_a, best_a)
        diagonal(i_b, j_b, score_b, best_b)
        hand_back(i, j)
        i_c, j_c = advance(i_b, j_b)
        got = prepare(i_c, j_c, got)
        scores_of(i_c, j_c, score_a, best_a)
        soften(i_b, j_b, score_b, best_b)
        diagonal(i_c, j_c, score_a, best_a)
        hand_back(i_b, j_b)
        return i_c, j_c, got

    units = jnp.int32(0)
    for which in range(2):
        for g in range(GROUPS):
            units = units + units_of(jnp.int32(which), jnp.int32(g))
    got = prepare(zero, zero, jnp.int32(1))
    scores_of(zero, zero, score_a, best_a)
    diagonal(zero, zero, score_a, best_a)
    lax.fori_loop(0, (units + 1) // 2, two_units, (zero, zero, got))

    pair_o.wait_recv()
    pair_s.wait_recv()
    peak = jnp.maximum(top[0], s_in[0:1, :])
    mine = jnp.exp2((top[0] - peak) * SCALE)
    other = jnp.exp2((s_in[0:1, :] - peak) * SCALE) * s_in[1:2, :]
    whole = mine * total[0] + other
    mine, other = mine / whole, other / whole
    for h in range(HEADS):
        part = slice(h * ROWS, (h + 1) * ROWS)
        merged = acc[0, :, part] * mine[:, part] + o_in[:, part].astype(jnp.float32) * other[:, part]
        o_ref[:, h * 128 : (h + 1) * 128] = merged.T.astype(jnp.bfloat16)

    own_each(lambda *a: own_copy(*a).wait_send(), lambda kind: None, FIRST + LAST)

    @pl.when(core == 0)
    def _():
        for way in range(2):
            for hop in range(4):
                for part in range(2):
                    if hop < 3 or part == way:
                        ring_copy(way, hop, part).wait_send()

    @pl.when(core == 1)
    def _():
        for g in range(GROUPS):
            for dx in range(1, 4):
                x_copy(jnp.int32(g), dx).wait_send()

    for g in range(GROUPS):
        core_copy(jnp.int32(g)).wait_send()
    pair_q.wait_send()
    pair_o.wait_send()
    pair_s.wait_send()


def body(queries, key_rows, value_rows, document_lengths):
    sems = pltpu.SemaphoreType.DMA
    vmem = pl.BlockSpec(memory_space=pltpu.VMEM)
    attended = pl.pallas_call(
        kernel,
        out_shape=jax.ShapeDtypeStruct((ROWS, HEADS * 128), jnp.bfloat16),
        in_specs=[pl.BlockSpec(memory_space=pltpu.SMEM)] + [pl.BlockSpec(memory_space=pl.ANY)] * 3,
        out_specs=vmem,
        scratch_shapes=[
            pltpu.VMEM((2, GROUPS, 2, 512, 128), jnp.bfloat16),
            pltpu.VMEM((GROUPS, 2, 512, 128), jnp.bfloat16),
            pltpu.VMEM((2, WIDE, 256), jnp.bfloat16),
            pltpu.VMEM((ROWS, HEADS * 128), jnp.bfloat16),
            pltpu.VMEM((ROWS, HEADS * 128), jnp.bfloat16),
            pltpu.VMEM((KEYS, WIDE), jnp.float32),
            pltpu.VMEM((KEYS, WIDE), jnp.float32),
            pltpu.VMEM((2, 128, WIDE), jnp.float32),
            pltpu.VMEM((2, 1, WIDE), jnp.float32),
            pltpu.VMEM((2, 1, WIDE), jnp.float32),
            pltpu.VMEM((1, WIDE), jnp.float32),
            pltpu.VMEM((1, WIDE), jnp.float32),
            pltpu.VMEM((128, WIDE), jnp.bfloat16),
            pltpu.VMEM((128, WIDE), jnp.bfloat16),
            pltpu.VMEM((8, WIDE), jnp.float32),
            pltpu.VMEM((8, WIDE), jnp.float32),
            sems((2, 4)), sems((1,)), sems((2, 8)), sems((8,)), sems((GROUPS, 4)), sems((GROUPS, 4)),
            sems((4, 2)), sems((4, 2)), sems((4, 2)), sems((4, 2)),
            sems((GROUPS,)), sems((GROUPS,)), sems((3,)), sems((3,)), sems,
        ],
        compiler_params=pltpu.CompilerParams(
            collective_id=0, has_side_effects=True, vmem_limit_bytes=63 * 2**20
        ),
        cost_estimate=pl.CostEstimate(flops=2 * 2 * 9216 * WIDE * 128, bytes_accessed=2**20, transcendentals=9216 * WIDE),
    )(document_lengths, queries[0], key_rows[0], value_rows[0])
    return attended[None]


def solution(mesh):
    in_specs = (
        P(None, "ctx", "head"),
        P(None, ("ctx", "head"), None),
        P(None, ("ctx", "head"), None),
        P(),
    )
    out_specs = P(None, "ctx", "head")
    return jax.shard_map(body, mesh=mesh, in_specs=in_specs, out_specs=out_specs, check_vma=False)
```
